512 devices in a mesh: ulysses: 8 (over z_hi, core), blk: 64 (over x, z_lo, y).
Axes of the slice: x: 4, y: 8, z: 8 (z_hi: 4, z_lo: 2; z = z_hi * 2 + z_lo), core: 2. Of those that a mesh axis runs over, the one named last changes fastest.
Arguments:
- queries: bfloat16 [65536, 1024], P(('blk', 'ulysses')), may hold values from -6 to 6
- key_rows: bfloat16 [65536, 1024], P(('blk', 'ulysses')), may hold values from -6 to 6
- value_rows: bfloat16 [65536, 1024], P(('blk', 'ulysses')), may hold values from -6 to 6
- attn_output: bfloat16 [65536, 1024], P(('blk', 'ulysses')), may hold values from -2 to 2
- grad_output: bfloat16 [65536, 1024], P(('blk', 'ulysses')), may hold values from -48 to 48
- logsumexp: float32 [65536, 8], P('blk', 'ulysses')
- positions: int32 [65536], replicated, may hold values from 0 to 4095, as said below
Outputs:
- grad_queries: bfloat16 [65536, 1024], P(('blk', 'ulysses'))
- grad_keys: bfloat16 [65536, 1024], P(('blk', 'ulysses'))
- grad_values: bfloat16 [65536, 1024], P(('blk', 'ulysses'))
The draws below stay inside these ranges and needn't reach their ends.
Inputs may be any that keep to these rules, and one draw needn't show every extreme that they name: For each s below 16, the runs s, s + 16, ..., s + 48 of 1024 rows hold one sequence of 4096 positions, each position once. Each such run holds, in order, the a-th and then the (7 - a)-th block of 512 consecutive positions, each ascending, with a different a for each run of the sequence.
All inputs are finite; a program needn't handle non-finite values.
Results may differ from the reference program's by a relative error of at most 0.0057.
Values may be sent and summed in bfloat16 or wider, within the bound.
No kernel may reach another device: no remote copies, remote signals or barrier semaphores. Data moves between devices by JAX's collectives and lax.ppermute only.
A program may use at most 64 MiB of HBM per device.

```python
import math
import jax
import jax.numpy as jnp
from jax import lax

HEAD_DIM = 128
SPAN = 4
TOK_BLK = 1024
HEADS = 8
SEQS = 16
LENGTH = 4096
TOKENS = 65536


def paired_rows(key):
    half_rows = TOK_BLK // 2
    raw_scores = jax.random.randint(jax.random.fold_in(key, 101), (SEQS, SPAN), 0, 1 << 20, dtype=jnp.int32)
    order_scores = raw_scores * SPAN + jnp.arange(SPAN, dtype=jnp.int32)[None, :]
    pair_order = jnp.argsort(order_scores, axis=1, stable=True).astype(jnp.int32)
    row_index = jnp.arange(TOKENS, dtype=jnp.int32)
    holder = row_index // TOK_BLK
    within = row_index % TOK_BLK
    second = within // half_rows
    offset = within % half_rows
    seq_of = holder % SEQS
    block_of = holder // SEQS
    pair_of = pair_order[seq_of, block_of]
    run_index = jnp.where(second == 0, pair_of, 2 * SPAN - 1 - pair_of)
    return (run_index * half_rows + offset).astype(jnp.int32)


def draw_positions(key, part):
    return paired_rows(key)


def draw_logsumexp(key, part):
    places = paired_rows(key)
    key = jax.random.fold_in(key, 7)
    centre = jnp.log(places.astype(jnp.float32) + 1.0) + 0.5
    jitter = jnp.clip(0.5 * jax.random.normal(key, (TOKENS, HEADS), jnp.float32), -1.0, 1.0)
    return centre[:, None] + jitter


def level_of(own_key, extent, shards, least, high):
    def one(dim, blocks):
        steps = jax.random.uniform(jax.random.fold_in(jax.random.fold_in(own_key, 6), dim), (blocks,), jnp.float32, least / len(shards), high / len(shards))
        return jnp.repeat(jnp.exp(steps), extent[dim] // blocks).reshape((-1,) + (1,) * (len(extent) - dim - 1))

    gain = one(*shards[0])
    for cut in shards[1:]:
        gain = gain * one(*cut)
    return gain


def bell_draw(stream_key, shape, spread, bound, cuts=(), kind=jnp.bfloat16):
    result = jax.random.normal(stream_key, shape, jnp.float32) * spread
    if len(cuts) > 0:
        result = level_of(stream_key, shape, cuts, -0.22, 0.18) * result
    return jnp.clip(result, min=-bound, max=bound).astype(kind)


def setup_inputs(seed: int = 0) -> dict:
    seeds = jax.random.split(jax.random.key(seed), 8)
    return {
        "queries": bell_draw(seeds[0], (TOKENS, HEADS * HEAD_DIM), 1.0, 6.0, ((0, 512),)),
        "key_rows": bell_draw(seeds[1], (TOKENS, HEADS * HEAD_DIM), 1.0, 6.0, ((0, 512),)),
        "value_rows": bell_draw(seeds[2], (TOKENS, HEADS * HEAD_DIM), 1.0, 6.0, ((0, 512),)),
        "attn_output": bell_draw(seeds[3], (TOKENS, HEADS * HEAD_DIM), 0.3, 2.0, ((0, 512),)),
        "grad_output": bell_draw(seeds[4], (TOKENS, HEADS * HEAD_DIM), 8.0, 48.0, ((0, 512),)),
        "logsumexp": draw_logsumexp(jax.random.fold_in(seeds[7], 71), 0),
        "positions": draw_positions(jax.random.fold_in(seeds[7], 71), 0),
    }


def head_grads(query_head, key_head, value_head, output_head, cotangent_head, lse_head, positions):
    scaling = HEAD_DIM ** -0.5
    block_rows = math.gcd(LENGTH, 512)
    block_count = LENGTH // block_rows
    delta_head = jnp.sum(cotangent_head.astype(jnp.float32) * output_head.astype(jnp.float32), axis=-1)

    def query_step(carry, blocks):
        grad_key_sum, grad_value_sum = carry
        query_block, cotangent_block, lse_block, delta_block, place_block = blocks
        scores = jnp.dot(query_block, key_head.T, preferred_element_type=jnp.float32) * scaling
        visible = place_block[:, None] >= positions[None, :]
        probs = jnp.where(visible, jnp.exp(scores - lse_block[:, None]), jnp.float32(0.0))
        probs_low = probs.astype(jnp.bfloat16)
        grad_value_sum = grad_value_sum + jnp.dot(probs_low.T, cotangent_block, preferred_element_type=jnp.float32)
        grad_probs = jnp.dot(cotangent_block, value_head.T, preferred_element_type=jnp.float32)
        grad_scores = (probs * (grad_probs - delta_block[:, None])).astype(jnp.bfloat16)
        grad_query_block = jnp.dot(grad_scores, key_head, preferred_element_type=jnp.float32) * scaling
        grad_key_sum = grad_key_sum + jnp.dot(grad_scores.T, query_block, preferred_element_type=jnp.float32) * scaling
        return (grad_key_sum, grad_value_sum), grad_query_block

    start_grads = (jnp.zeros((LENGTH, HEAD_DIM), jnp.float32), jnp.zeros((LENGTH, HEAD_DIM), jnp.float32))
    blocks = (query_head.reshape(block_count, block_rows, HEAD_DIM),
              cotangent_head.reshape(block_count, block_rows, HEAD_DIM),
              lse_head.reshape(block_count, block_rows),
              delta_head.reshape(block_count, block_rows),
              positions.reshape(block_count, block_rows))
    (grad_key_sum, grad_value_sum), grad_query_blocks = lax.scan(query_step, start_grads, blocks)
    return grad_query_blocks.reshape(LENGTH, HEAD_DIM), grad_key_sum, grad_value_sum


def to_sequences(matrix):
    width = matrix.shape[-1]
    return matrix.reshape(SPAN, SEQS, TOK_BLK, width).transpose(1, 0, 2, 3).reshape(SEQS, LENGTH, width)


def from_sequences(stacked):
    width = stacked.shape[-1]
    return stacked.reshape(SEQS, SPAN, TOK_BLK, width).transpose(1, 0, 2, 3).reshape(TOKENS, width)


def split_heads(matrix):
    return matrix.reshape(LENGTH, HEADS, HEAD_DIM).transpose(1, 0, 2)


def join_heads(stacked):
    return stacked.transpose(1, 0, 2).reshape(LENGTH, HEADS * HEAD_DIM).astype(jnp.bfloat16)


def one_sequence(members):
    query_seq, key_seq, value_seq, output_seq, cotangent_seq, lse_seq, place_seq = members

    def one_head(parts):
        return head_grads(parts[0], parts[1], parts[2], parts[3], parts[4], parts[5], place_seq)

    grad_query_all, grad_key_all, grad_value_all = lax.map(
        one_head,
        (split_heads(query_seq), split_heads(key_seq), split_heads(value_seq),
         split_heads(output_seq), split_heads(cotangent_seq), lse_seq.T))
    return join_heads(grad_query_all), join_heads(grad_key_all), join_heads(grad_value_all)


def reference(queries, key_rows, value_rows, attn_output, grad_output, logsumexp, positions):
    place_seqs = positions.reshape(SPAN, SEQS, TOK_BLK).transpose(1, 0, 2).reshape(SEQS, LENGTH)
    grad_query_seqs, grad_key_seqs, grad_value_seqs = lax.map(
        one_sequence,
        (to_sequences(queries), to_sequences(key_rows), to_sequences(value_rows),
         to_sequences(attn_output), to_sequences(grad_output), to_sequences(logsumexp), place_seqs))
    return from_sequences(grad_query_seqs), from_sequences(grad_key_seqs), from_sequences(grad_value_seqs)
```

```python
import functools

import jax
import jax.numpy as jnp
from jax import lax
from jax.experimental import pallas as pl
from jax.experimental.pallas import tpu as pltpu
from jax.sharding import PartitionSpec as P

SPAN = 4
HEAD_DIM = 128
LOG2E = 1.4426950408889634
SCALE = HEAD_DIM ** -0.5
ROWS = 128
OWNERS = 8
HALF = OWNERS // 2
EXTRA = 16
TILE = 2
KTILE = 2
f32 = jnp.float32
bf16 = jnp.bfloat16
VMEM = pl.BlockSpec(memory_space=pltpu.VMEM)
SMEM = pl.BlockSpec(memory_space=pltpu.SMEM)
PARAMS = pltpu.CompilerParams(vmem_limit_bytes=48 * 1024 * 1024)


def three_terms(row):
    high = row.astype(bf16).astype(f32)
    rest = row - high
    middle = rest.astype(bf16).astype(f32)
    return (high, middle, rest - middle)


def pack_kernel(query_ref, key_ref, value_ref, output_ref, cotangent_ref, packed_ref):
    place = lax.broadcasted_iota(jnp.int32, (EXTRA, ROWS), 0)
    for head in range(OWNERS):
        columns = pl.ds(head * HEAD_DIM, HEAD_DIM)
        cotangent = cotangent_ref[:, columns]
        packed_ref[head, 0:128, :] = query_ref[:, columns]
        packed_ref[head, 128:256, :] = cotangent
        packed_ref[head, 256:384, :] = key_ref[:, columns]
        packed_ref[head, 384:512, :] = value_ref[:, columns]
        product = cotangent.astype(f32) * output_ref[:, columns].astype(f32)
        delta = jnp.sum(product.T, axis=0, keepdims=True)
        high, middle, low = three_terms(delta)
        rows = jnp.where(
            place == 0, high, jnp.where(place == 1, middle, jnp.where(place == 2, low, 0.0))
        )
        packed_ref[head, 512:528, :] = rows.astype(bf16)


def split_kernel(moved_ref, lse_ref, query_side_ref, key_side_ref):
    place = lax.broadcasted_iota(jnp.int32, (EXTRA, ROWS), 0)
    for owner in range(OWNERS):
        query_side_ref[owner, 0:256, :] = moved_ref[owner, 0:256, :]
        key_side_ref[owner] = moved_ref[owner, 256:512, :]
        high, middle, low = three_terms(lse_ref[owner : owner + 1, :])
        rows = moved_ref[owner, 512:528, :].astype(f32)
        rows = jnp.where(
            place == 3, high, jnp.where(place == 4, middle, jnp.where(place == 5, low, rows))
        )
        query_side_ref[owner, 256:272, :] = rows.astype(bf16)


def read_rows(query_side_ref, lse_ref, delta_ref):
    for owner in range(OWNERS):
        rows = query_side_ref[owner, 256:272, :].astype(f32)
        delta = rows[0:1] + rows[1:2] + rows[2:3]
        lse = rows[3:4] + rows[4:5] + rows[5:6]
        group, part = owner // TILE, owner % TILE
        delta_ref[group, :, part * ROWS : (part + 1) * ROWS] = delta
        lse_ref[group, :, part * ROWS : (part + 1) * ROWS] = lse * LOG2E


def nt(left, right):
    return lax.dot_general(left, right, (((1,), (1,)), ((), ())), preferred_element_type=f32)


def nn(left, right):
    return lax.dot_general(left, right, (((1,), (0,)), ((), ())), preferred_element_type=f32)


def tn(left, right):
    return lax.dot_general(left, right, (((0,), (0,)), ((), ())), preferred_element_type=f32)


def block_grads(query_half, key_half, query_refs, key_refs, diagonal):
    query_side_ref, lse_ref, delta_ref, grad_query_ref = query_refs
    key_side_ref, grad_key_ref, grad_value_ref = key_refs
    query_rows, key_rows = TILE * ROWS, KTILE * ROWS
    for key_tile in range(HALF // KTILE):
        keys_at = pl.ds(key_half * HALF + key_tile * KTILE, KTILE)
        key = key_side_ref[keys_at, 0:128, :].reshape(key_rows, HEAD_DIM)
        value = key_side_ref[keys_at, 128:256, :].reshape(key_rows, HEAD_DIM)
        grad_key = grad_key_ref[keys_at].reshape(key_rows, HEAD_DIM)
        grad_value = grad_value_ref[keys_at].reshape(key_rows, HEAD_DIM)
        for query_tile in range(HALF // TILE):
            first_query = query_tile * query_rows
            first_key = key_tile * key_rows
            if diagonal and first_query + query_rows <= first_key:
                continue
            queries_at = pl.ds(query_half * HALF + query_tile * TILE, TILE)
            group = query_half * (HALF // TILE) + query_tile
            query = query_side_ref[queries_at, 0:128, :].reshape(query_rows, HEAD_DIM)
            cotangent = query_side_ref[queries_at, 128:256, :].reshape(query_rows, HEAD_DIM)
            scores = nt(key, query)
            probs = jnp.exp2(scores * (SCALE * LOG2E) - lse_ref[group])
            if diagonal and first_query < first_key + key_rows - 1:
                key_place = first_key + lax.broadcasted_iota(jnp.int32, probs.shape, 0)
                query_place = first_query + lax.broadcasted_iota(jnp.int32, probs.shape, 1)
                probs = jnp.where(query_place >= key_place, probs, 0.0)
            grad_probs = nt(value, cotangent)
            grad_scores = (probs * (grad_probs - delta_ref[group])).astype(bf16)
            grad_value += nn(probs.astype(bf16), cotangent)
            grad_key += nn(grad_scores, query)
            grad_query = tn(grad_scores, key)
            grad_query_ref[queries_at] += grad_query.reshape(TILE, ROWS, HEAD_DIM)
        grad_key_ref[keys_at] = grad_key.reshape(KTILE, ROWS, HEAD_DIM)
        grad_value_ref[keys_at] = grad_value.reshape(KTILE, ROWS, HEAD_DIM)


def own_kernel(
    query_side_ref, key_side_ref, grad_query_ref, grad_key_ref, grad_value_ref, lse_ref, delta_ref
):
    grad_query_ref[...] = jnp.zeros_like(grad_query_ref)
    grad_key_ref[...] = jnp.zeros_like(grad_key_ref)
    grad_value_ref[...] = jnp.zeros_like(grad_value_ref)
    read_rows(query_side_ref, lse_ref, delta_ref)
    query_refs = (query_side_ref, lse_ref, delta_ref, grad_query_ref)
    key_refs = (key_side_ref, grad_key_ref, grad_value_ref)
    block_grads(1, 0, query_refs, key_refs, False)
    block_grads(0, 0, query_refs, key_refs, True)
    block_grads(1, 1, query_refs, key_refs, True)


def cross_kernel(
    halves_ref,
    query_side_ref,
    key_side_ref,
    far_query_side_ref,
    far_key_side_ref,
    first_query_ref,
    first_key_ref,
    first_value_ref,
    grad_query_ref,
    grad_key_ref,
    grad_value_ref,
    far_grad_query_ref,
    far_grad_pair_ref,
    lse_ref,
    delta_ref,
    far_lse_ref,
    far_delta_ref,
    far_query_sum,
    far_key_sum,
    far_value_sum,
):
    grad_query_ref[...] = first_query_ref[...]
    grad_key_ref[...] = first_key_ref[...]
    grad_value_ref[...] = first_value_ref[...]
    far_query_sum[...] = jnp.zeros_like(far_query_sum)
    far_key_sum[...] = jnp.zeros_like(far_key_sum)
    far_value_sum[...] = jnp.zeros_like(far_value_sum)
    read_rows(query_side_ref, lse_ref, delta_ref)
    read_rows(far_query_side_ref, far_lse_ref, far_delta_ref)
    near_query = (query_side_ref, lse_ref, delta_ref, grad_query_ref)
    far_query = (far_query_side_ref, far_lse_ref, far_delta_ref, far_query_sum)
    near_key = (key_side_ref, grad_key_ref, grad_value_ref)
    far_key = (far_key_side_ref, far_key_sum, far_value_sum)
    for index, (query_refs, key_refs) in enumerate(
        ((far_query, far_key), (near_query, far_key), (far_query, near_key))
    ):
        half = halves_ref[index]
        block_grads(1, 0, query_refs, key_refs, False)
        block_grads(half, half, query_refs, key_refs, False)
    grad_query_ref[...] = grad_query_ref[...] * SCALE
    grad_key_ref[...] = grad_key_ref[...] * SCALE
    far_grad_query_ref[...] = (far_query_sum[...] * SCALE).astype(bf16)
    far_grad_pair_ref[0] = (far_key_sum[...] * SCALE).astype(bf16)
    far_grad_pair_ref[1] = far_value_sum[...].astype(bf16)


def join_kernel(
    grad_query_ref, grad_key_ref, grad_value_ref, back_query_ref, back_pair_ref, packed_ref
):
    packed_ref[:, 0:128, :] = (grad_query_ref[...] + back_query_ref[...].astype(f32)).astype(bf16)
    packed_ref[:, 128:256, :] = (grad_key_ref[...] + back_pair_ref[0].astype(f32)).astype(bf16)
    packed_ref[:, 256:384, :] = (grad_value_ref[...] + back_pair_ref[1].astype(f32)).astype(bf16)


def unpack_kernel(moved_ref, grad_query_ref, grad_key_ref, grad_value_ref):
    for head in range(OWNERS):
        columns = pl.ds(head * HEAD_DIM, HEAD_DIM)
        grad_query_ref[:, columns] = moved_ref[head, 0:128, :]
        grad_key_ref[:, columns] = moved_ref[head, 128:256, :]
        grad_value_ref[:, columns] = moved_ref[head, 256:384, :]


def call(kernel, args, specs, outs, scratch=(), flops=0, moved=4 << 20, name=None):
    return pl.pallas_call(
        kernel,
        out_shape=[jax.ShapeDtypeStruct(shape, dtype) for shape, dtype in outs],
        in_specs=specs,
        out_specs=[VMEM] * len(outs),
        scratch_shapes=list(scratch),
        compiler_params=PARAMS,
        cost_estimate=pl.CostEstimate(flops=flops, bytes_accessed=moved, transcendentals=0),
        name=name,
    )(*args)


def row_scratch():
    return pltpu.VMEM((OWNERS // TILE, 1, TILE * ROWS), f32)


def per_device(queries, key_rows, value_rows, attn_output, grad_output, logsumexp, positions):
    blk_count = lax.axis_size("blk")
    stride = blk_count // SPAN
    run_rows = logsumexp.shape[0]
    here = lax.axis_index("blk")
    place, line = here // stride, here % stride
    query_mate = lambda at: at ^ 1
    key_mate = lambda at: SPAN - 1 - at

    def swapped(value, mate):
        pairs = [(b, mate(b // stride) * stride + b % stride) for b in range(blk_count)]
        return lax.ppermute(value, "blk", pairs)

    def first_place(at):
        start = (at * stride + line) * run_rows
        return lax.dynamic_slice_in_dim(positions, start, 1)

    own_first = first_place(place)
    query_first = first_place(query_mate(place))
    key_first = first_place(key_mate(place))
    halves = jnp.concatenate(
        [query_first < key_first, own_first < key_first, query_first < own_first]
    ).astype(jnp.int32)

    side = (OWNERS, ROWS, HEAD_DIM)
    (packed,) = call(
        pack_kernel,
        (queries, key_rows, value_rows, attn_output, grad_output),
        [VMEM] * 5,
        [((OWNERS, 528, HEAD_DIM), bf16)],
        name="pack",
    )
    moved = lax.all_to_all(packed, "ulysses", split_axis=0, concat_axis=0, tiled=True)
    query_side, key_side = call(
        split_kernel,
        (moved, logsumexp.reshape(OWNERS, ROWS)),
        [VMEM] * 2,
        [((OWNERS, 272, HEAD_DIM), bf16), ((OWNERS, 256, HEAD_DIM), bf16)],
        name="split",
    )
    far_query_side = swapped(query_side, query_mate)
    far_key_side = swapped(key_side, key_mate)
    own = call(
        own_kernel,
        (query_side, key_side),
        [VMEM] * 2,
        [(side, f32)] * 3,
        [row_scratch(), row_scratch()],
        flops=10 * 128 * 10 * 256 * 256,
        name="own",
    )
    grad_query, grad_key, grad_value, far_grad_query, far_grad_pair = call(
        cross_kernel,
        (halves, query_side, key_side, far_query_side, far_key_side, *own),
        [SMEM] + [VMEM] * 7,
        [(side, f32)] * 3 + [(side, bf16), ((2,) + side, bf16)],
        [row_scratch() for _ in range(4)] + [pltpu.VMEM(side, f32) for _ in range(3)],
        flops=10 * 128 * 24 * 256 * 256,
        name="cross",
    )
    back_query = swapped(far_grad_query, query_mate)
    back_pair = swapped(far_grad_pair, key_mate)
    (joined,) = call(
        join_kernel,
        (grad_query, grad_key, grad_value, back_query, back_pair),
        [VMEM] * 5,
        [((OWNERS, 384, HEAD_DIM), bf16)],
        name="join",
    )
    returned = lax.all_to_all(joined, "ulysses", split_axis=0, concat_axis=0, tiled=True)
    return tuple(
        call(
            unpack_kernel,
            (returned,),
            [VMEM],
            [((ROWS, OWNERS * HEAD_DIM), bf16)] * 3,
            name="unpack",
        )
    )


def solution(mesh):
    tokens = P(("blk", "ulysses"), None)
    return jax.shard_map(
        per_device,
        mesh=mesh,
        in_specs=(tokens,) * 5 + (P("blk", "ulysses"), P()),
        out_specs=(tokens,) * 3,
        check_vma=False,
    )
```

```python
import functools

import jax
import jax.numpy as jnp
from jax import lax
from jax.experimental import pallas as pl
from jax.experimental.pallas import tpu as pltpu
from jax.sharding import PartitionSpec as P

SPAN = 4
HEAD_DIM = 128
LOG2E = 1.4426950408889634
SCALE = HEAD_DIM ** -0.5
ROWS = 128
OWNERS = 8
HALF = OWNERS // 2
EXTRA = 16
TILE = 2
KTILE = 2
f32 = jnp.float32
bf16 = jnp.bfloat16
VMEM = pl.BlockSpec(memory_space=pltpu.VMEM)
HBM = pl.BlockSpec(memory_space=pltpu.HBM)
SMEM = pl.BlockSpec(memory_space=pltpu.SMEM)
PARAMS = pltpu.CompilerParams(vmem_limit_bytes=48 * 1024 * 1024)


def three_terms(row):
    high = row.astype(bf16).astype(f32)
    rest = row - high
    middle = rest.astype(bf16).astype(f32)
    return (high, middle, rest - middle)


def pack_kernel(
    query_ref, key_ref, value_ref, output_ref, cotangent_ref, packed_ref, output_here, arrived
):
    def copies(index, source):
        for head in range(OWNERS):
            columns = pl.ds(head * HEAD_DIM, HEAD_DIM)
            target = output_here.at[head]
            if index < 4:
                target = packed_ref.at[head, pl.ds(index * ROWS, ROWS), :]
            yield pltpu.make_async_copy(source.at[:, columns], target, arrived.at[index, head])

    sources = (query_ref, cotangent_ref, key_ref, value_ref, output_ref)
    moves = [list(copies(index, source)) for index, source in enumerate(sources)]
    for index in (1, 4, 0, 2, 3):
        for move in moves[index]:
            move.start()
    place = lax.broadcasted_iota(jnp.int32, (EXTRA, ROWS), 0)
    for head in range(OWNERS):
        moves[1][head].wait()
        moves[4][head].wait()
        product = packed_ref[head, 128:256, :].astype(f32) * output_here[head].astype(f32)
        delta = jnp.sum(product.T, axis=0, keepdims=True)
        high, middle, low = three_terms(delta)
        rows = jnp.where(
            place == 0, high, jnp.where(place == 1, middle, jnp.where(place == 2, low, 0.0))
        )
        packed_ref[head, 512:528, :] = rows.astype(bf16)
    for index in (0, 2, 3):
        for move in moves[index]:
            move.wait()


def split_kernel(moved_ref, lse_ref, query_side_ref, key_side_ref):
    place = lax.broadcasted_iota(jnp.int32, (EXTRA, ROWS), 0)
    for owner in range(OWNERS):
        query_side_ref[owner, 0:256, :] = moved_ref[owner, 0:256, :]
        key_side_ref[owner] = moved_ref[owner, 256:512, :]
        high, middle, low = three_terms(lse_ref[owner : owner + 1, :])
        rows = moved_ref[owner, 512:528, :].astype(f32)
        rows = jnp.where(
            place == 3, high, jnp.where(place == 4, middle, jnp.where(place == 5, low, rows))
        )
        query_side_ref[owner, 256:272, :] = rows.astype(bf16)


def read_rows(query_side_ref, lse_ref, delta_ref):
    for owner in range(OWNERS):
        rows = query_side_ref[owner, 256:272, :].astype(f32)
        delta = rows[0:1] + rows[1:2] + rows[2:3]
        lse = rows[3:4] + rows[4:5] + rows[5:6]
        group, part = owner // TILE, owner % TILE
        delta_ref[group, :, part * ROWS : (part + 1) * ROWS] = delta
        lse_ref[group, :, part * ROWS : (part + 1) * ROWS] = lse * LOG2E


def nt(left, right):
    return lax.dot_general(left, right, (((1,), (1,)), ((), ())), preferred_element_type=f32)


def nn(left, right):
    return lax.dot_general(left, right, (((1,), (0,)), ((), ())), preferred_element_type=f32)


def tn(left, right):
    return lax.dot_general(left, right, (((0,), (0,)), ((), ())), preferred_element_type=f32)


def block_grads(query_half, key_half, query_refs, key_refs, diagonal):
    query_side_ref, lse_ref, delta_ref, grad_query_ref = query_refs
    key_side_ref, grad_key_ref, grad_value_ref = key_refs
    query_rows, key_rows = TILE * ROWS, KTILE * ROWS
    for key_tile in range(HALF // KTILE):
        keys_at = pl.ds(key_half * HALF + key_tile * KTILE, KTILE)
        key = key_side_ref[keys_at, 0:128, :].reshape(key_rows, HEAD_DIM)
        value = key_side_ref[keys_at, 128:256, :].reshape(key_rows, HEAD_DIM)
        grad_key = grad_key_ref[keys_at].reshape(key_rows, HEAD_DIM)
        grad_value = grad_value_ref[keys_at].reshape(key_rows, HEAD_DIM)
        for query_tile in range(HALF // TILE):
            first_query = query_tile * query_rows
            first_key = key_tile * key_rows
            if diagonal and first_query + query_rows <= first_key:
                continue
            queries_at = pl.ds(query_half * HALF + query_tile * TILE, TILE)
            group = query_half * (HALF // TILE) + query_tile
            query = query_side_ref[queries_at, 0:128, :].reshape(query_rows, HEAD_DIM)
            cotangent = query_side_ref[queries_at, 128:256, :].reshape(query_rows, HEAD_DIM)
            scores = nt(key, query)
            probs = jnp.exp2(scores * (SCALE * LOG2E) - lse_ref[group])
            if diagonal and first_query < first_key + key_rows - 1:
                key_place = first_key + lax.broadcasted_iota(jnp.int32, probs.shape, 0)
                query_place = first_query + lax.broadcasted_iota(jnp.int32, probs.shape, 1)
                probs = jnp.where(query_place >= key_place, probs, 0.0)
            grad_probs = nt(value, cotangent)
            grad_scores = (probs * (grad_probs - delta_ref[group])).astype(bf16)
            grad_value += nn(probs.astype(bf16), cotangent)
            grad_key += nn(grad_scores, query)
            grad_query = tn(grad_scores, key)
            grad_query_ref[queries_at] += grad_query.reshape(TILE, ROWS, HEAD_DIM)
        grad_key_ref[keys_at] = grad_key.reshape(KTILE, ROWS, HEAD_DIM)
        grad_value_ref[keys_at] = grad_value.reshape(KTILE, ROWS, HEAD_DIM)


def own_kernel(
    query_side_ref, key_side_ref, grad_query_ref, grad_key_ref, grad_value_ref, lse_ref, delta_ref
):
    grad_query_ref[...] = jnp.zeros_like(grad_query_ref)
    grad_key_ref[...] = jnp.zeros_like(grad_key_ref)
    grad_value_ref[...] = jnp.zeros_like(grad_value_ref)
    read_rows(query_side_ref, lse_ref, delta_ref)
    query_refs = (query_side_ref, lse_ref, delta_ref, grad_query_ref)
    key_refs = (key_side_ref, grad_key_ref, grad_value_ref)
    block_grads(1, 0, query_refs, key_refs, False)
    block_grads(0, 0, query_refs, key_refs, True)
    block_grads(1, 1, query_refs, key_refs, True)


def pair_grads(half, query_refs, key_refs):
    block_grads(1, 0, query_refs, key_refs, False)
    block_grads(half, half, query_refs, key_refs, False)


def near_far_kernel(
    halves_ref,
    query_side_ref,
    far_key_side_ref,
    first_query_ref,
    grad_query_ref,
    far_key_ref,
    far_value_ref,
    lse_ref,
    delta_ref,
):
    grad_query_ref[...] = first_query_ref[...]
    far_key_ref[...] = jnp.zeros_like(far_key_ref)
    far_value_ref[...] = jnp.zeros_like(far_value_ref)
    read_rows(query_side_ref, lse_ref, delta_ref)
    near_query = (query_side_ref, lse_ref, delta_ref, grad_query_ref)
    pair_grads(halves_ref[1], near_query, (far_key_side_ref, far_key_ref, far_value_ref))
    grad_query_ref[...] = grad_query_ref[...] * SCALE


def far_far_kernel(
    halves_ref,
    far_query_side_ref,
    far_key_side_ref,
    first_key_ref,
    first_value_ref,
    far_query_ref,
    far_pair_ref,
    lse_ref,
    delta_ref,
    far_key_sum,
    far_value_sum,
):
    far_query_ref[...] = jnp.zeros_like(far_query_ref)
    far_key_sum[...] = first_key_ref[...]
    far_value_sum[...] = first_value_ref[...]
    read_rows(far_query_side_ref, lse_ref, delta_ref)
    far_query = (far_query_side_ref, lse_ref, delta_ref, far_query_ref)
    pair_grads(halves_ref[0], far_query, (far_key_side_ref, far_key_sum, far_value_sum))
    far_pair_ref[0] = (far_key_sum[...] * SCALE).astype(bf16)
    far_pair_ref[1] = far_value_sum[...].astype(bf16)


def far_near_kernel(
    halves_ref,
    far_query_side_ref,
    key_side_ref,
    first_query_ref,
    first_key_ref,
    first_value_ref,
    far_query_ref,
    grad_key_ref,
    grad_value_ref,
    lse_ref,
    delta_ref,
    far_query_sum,
):
    far_query_sum[...] = first_query_ref[...]
    grad_key_ref[...] = first_key_ref[...]
    grad_value_ref[...] = first_value_ref[...]
    read_rows(far_query_side_ref, lse_ref, delta_ref)
    far_query = (far_query_side_ref, lse_ref, delta_ref, far_query_sum)
    pair_grads(halves_ref[2], far_query, (key_side_ref, grad_key_ref, grad_value_ref))
    grad_key_ref[...] = grad_key_ref[...] * SCALE
    far_query_ref[...] = (far_query_sum[...] * SCALE).astype(bf16)


def join_kernel(
    grad_query_ref, grad_key_ref, grad_value_ref, back_query_ref, back_pair_ref, packed_ref
):
    packed_ref[:, 0:128, :] = (grad_query_ref[...] + back_query_ref[...].astype(f32)).astype(bf16)
    packed_ref[:, 128:256, :] = (grad_key_ref[...] + back_pair_ref[0].astype(f32)).astype(bf16)
    packed_ref[:, 256:384, :] = (grad_value_ref[...] + back_pair_ref[1].astype(f32)).astype(bf16)


def unpack_kernel(moved_ref, grad_query_ref, grad_key_ref, grad_value_ref, sent):
    moves = []
    for head in range(OWNERS):
        columns = pl.ds(head * HEAD_DIM, HEAD_DIM)
        for index, target in enumerate((grad_query_ref, grad_key_ref, grad_value_ref)):
            source = moved_ref.at[head, pl.ds(index * ROWS, ROWS), :]
            moves.append(
                pltpu.make_async_copy(source, target.at[:, columns], sent.at[index, head])
            )
    for move in moves:
        move.start()
    for move in moves:
        move.wait()


def call(kernel, args, specs, outs, scratch=(), flops=0, moved=4 << 20, name=None, space=VMEM):
    return pl.pallas_call(
        kernel,
        out_shape=[jax.ShapeDtypeStruct(shape, dtype) for shape, dtype in outs],
        in_specs=specs,
        out_specs=[space] * len(outs),
        scratch_shapes=list(scratch),
        compiler_params=PARAMS,
        cost_estimate=pl.CostEstimate(flops=flops, bytes_accessed=moved, transcendentals=0),
        name=name,
    )(*args)


def row_scratch():
    return pltpu.VMEM((OWNERS // TILE, 1, TILE * ROWS), f32)


def per_device(queries, key_rows, value_rows, attn_output, grad_output, logsumexp, positions):
    blk_count = lax.axis_size("blk")
    stride = blk_count // SPAN
    run_rows = logsumexp.shape[0]
    here = lax.axis_index("blk")
    place, line = here // stride, here % stride
    query_mate = lambda at: at ^ 1
    key_mate = lambda at: SPAN - 1 - at

    def swapped(value, mate):
        pairs = [(b, mate(b // stride) * stride + b % stride) for b in range(blk_count)]
        return lax.ppermute(value, "blk", pairs)

    def first_place(at):
        start = (at * stride + line) * run_rows
        return lax.dynamic_slice_in_dim(positions, start, 1)

    own_first = first_place(place)
    query_first = first_place(query_mate(place))
    key_first = first_place(key_mate(place))
    halves = jnp.concatenate(
        [query_first < key_first, own_first < key_first, query_first < own_first]
    ).astype(jnp.int32)

    side = (OWNERS, ROWS, HEAD_DIM)
    (packed,) = call(
        pack_kernel,
        tuple(pltpu.with_memory_space_constraint(x, pltpu.HBM) for x in (queries, key_rows, value_rows, attn_output, grad_output)),
        [HBM] * 5,
        [((OWNERS, 528, HEAD_DIM), bf16)],
        [pltpu.VMEM((OWNERS, ROWS, HEAD_DIM), bf16), pltpu.SemaphoreType.DMA((5, OWNERS))],
        name="pack",
    )
    moved = lax.all_to_all(packed, "ulysses", split_axis=0, concat_axis=0, tiled=True)
    query_side, key_side = call(
        split_kernel,
        (moved, logsumexp.reshape(OWNERS, ROWS)),
        [VMEM] * 2,
        [((OWNERS, 272, HEAD_DIM), bf16), ((OWNERS, 256, HEAD_DIM), bf16)],
        name="split",
    )
    far_key_side = swapped(key_side, key_mate)
    far_query_side = swapped(query_side, query_mate)
    own = call(
        own_kernel,
        (query_side, key_side),
        [VMEM] * 2,
        [(side, f32)] * 3,
        [row_scratch(), row_scratch()],
        flops=10 * 128 * 10 * 256 * 256,
        name="own",
    )
    cost = 10 * 128 * 8 * 256 * 256
    grad_query, first_far_key, first_far_value = call(
        near_far_kernel,
        (halves, query_side, far_key_side, own[0]),
        [SMEM] + [VMEM] * 3,
        [(side, f32)] * 3,
        [row_scratch(), row_scratch()],
        flops=cost,
        name="near_far",
    )
    first_far_query, far_grad_pair = call(
        far_far_kernel,
        (halves, far_query_side, far_key_side, first_far_key, first_far_value),
        [SMEM] + [VMEM] * 4,
        [(side, f32), ((2,) + side, bf16)],
        [row_scratch(), row_scratch(), pltpu.VMEM(side, f32), pltpu.VMEM(side, f32)],
        flops=cost,
        name="far_far",
    )
    back_pair = swapped(far_grad_pair, key_mate)
    far_grad_query, grad_key, grad_value = call(
        far_near_kernel,
        (halves, far_query_side, key_side, first_far_query, own[1], own[2]),
        [SMEM] + [VMEM] * 5,
        [(side, bf16), (side, f32), (side, f32)],
        [row_scratch(), row_scratch(), pltpu.VMEM(side, f32)],
        flops=cost,
        name="far_near",
    )
    back_query = swapped(far_grad_query, query_mate)
    (joined,) = call(
        join_kernel,
        (grad_query, grad_key, grad_value, back_query, back_pair),
        [VMEM] * 5,
        [((OWNERS, 384, HEAD_DIM), bf16)],
        name="join",
    )
    returned = lax.all_to_all(joined, "ulysses", split_axis=0, concat_axis=0, tiled=True)
    return tuple(
        call(
            unpack_kernel,
            (returned,),
            [VMEM],
            [((ROWS, OWNERS * HEAD_DIM), bf16)] * 3,
            [pltpu.SemaphoreType.DMA((3, OWNERS))],
            name="unpack",
            space=HBM,
        )
    )


def solution(mesh):
    tokens = P(("blk", "ulysses"), None)
    return jax.shard_map(
        per_device,
        mesh=mesh,
        in_specs=(tokens,) * 5 + (P("blk", "ulysses"), P()),
        out_specs=(tokens,) * 3,
        check_vma=False,
    )
```

```python
import jax
import jax.numpy as jnp
from jax import lax
from jax.experimental import pallas as pl
from jax.experimental.pallas import tpu as pltpu
from jax.sharding import PartitionSpec as P

SPAN = 4
HEAD_DIM = 128
LOG2E = 1.4426950408889634
SCALE = HEAD_DIM ** -0.5
ROWS = 128
HEADS = 8
OWNERS = 8
HALF = 4
CHUNK = 256
EXTRA = 16
PART = 4 * ROWS + EXTRA
AXES = ("ulysses", "blk")
f32 = jnp.float32
bf16 = jnp.bfloat16
VMEM = pl.BlockSpec(memory_space=pltpu.VMEM)
SMEM = pl.BlockSpec(memory_space=pltpu.SMEM)
HBM = pl.BlockSpec(memory_space=pltpu.HBM)
PARAMS = pltpu.CompilerParams(vmem_limit_bytes=24 * 1024 * 1024)


def three_terms(row):
    high = row.astype(bf16).astype(f32)
    rest = row - high
    middle = rest.astype(bf16).astype(f32)
    return (high, middle, rest - middle)


def chunk_at(level, pair):
    return jnp.where(
        level == 0,
        2 * pair,
        jnp.where(level == 1, 2 * pair + 1, jnp.where(level == 2, 14 - 2 * pair, 15 - 2 * pair)),
    )


def rank_at(level, pair):
    return jnp.where(level < 2, pair, 3 - pair)


def fill_table(table_ref, pairs, role, place, level):
    def pick(at):
        value = pairs[0]
        for index in range(1, SPAN):
            value = jnp.where(at == index, pairs[index], value)
        return value

    sides = ((place, level), (SPAN - 1 - place, level ^ 1), (place ^ 1, 3 - level))
    for side, (run, height) in enumerate(sides):
        pair = pick(run)
        for index in range(4):
            over_x = chunk_at(jnp.int32(index), pair)
            over_z = 2 * index + jnp.where(height < 2, height, height + 6)
            table_ref[4 * side + index] = jnp.where(role == 0, over_x, over_z)
    for slot in range(SPAN):
        table_ref[12 + slot] = jnp.where(role == 0, slot, rank_at(level, pairs[slot]))
        table_ref[16 + slot] = pairs[slot]


def pack_kernel(
    where_ref,
    query_ref,
    key_ref,
    value_ref,
    output_ref,
    cotangent_ref,
    positions_ref,
    packed_ref,
    table_ref,
    output_here,
    places,
    arrived,
    places_arrived,
):
    role, place, level, line, stride = (where_ref[index] for index in range(5))
    run_rows = OWNERS * ROWS
    first_places = []
    for run in range(SPAN):
        start = pl.multiple_of((run * stride + line) * run_rows, run_rows)
        first_places.append(
            pltpu.make_async_copy(
                positions_ref.at[pl.ds(start, 128)], places.at[run], places_arrived.at[run]
            )
        )

    def copies(index, source):
        for head in range(HEADS):
            columns = pl.ds(head * HEAD_DIM, HEAD_DIM)
            target = output_here.at[head]
            if index < 4:
                target = packed_ref.at[head % 2, head // 2, pl.ds(index * ROWS, ROWS), :]
            yield pltpu.make_async_copy(source.at[:, columns], target, arrived.at[index, head])

    sources = (query_ref, cotangent_ref, key_ref, value_ref, output_ref)
    moves = [list(copies(index, source)) for index, source in enumerate(sources)]
    for index in (1, 4, 0, 2, 3):
        for move in moves[index]:
            move.start()
    for move in first_places:
        move.start()
    row = lax.broadcasted_iota(jnp.int32, (EXTRA, ROWS), 0)
    for head in range(HEADS):
        moves[1][head].wait()
        moves[4][head].wait()
        cotangent = packed_ref[head % 2, head // 2, 128:256, :].astype(f32)
        delta = jnp.sum((cotangent * output_here[head].astype(f32)).T, axis=0, keepdims=True)
        high, middle, low = three_terms(delta)
        rows = jnp.where(row == 0, high, jnp.where(row == 1, middle, jnp.where(row == 2, low, 0.0)))
        packed_ref[head % 2, head // 2, 512:528, :] = rows.astype(bf16)
    for move in first_places:
        move.wait()
    pairs = [
        jnp.minimum(lax.div(places[run, 0], jnp.int32(2 * CHUNK)), SPAN - 1) for run in range(SPAN)
    ]
    fill_table(table_ref, pairs, role, place, level)
    for index in (0, 2, 3):
        for move in moves[index]:
            move.wait()


def with_lse(rows, lse):
    row = lax.broadcasted_iota(jnp.int32, (EXTRA, ROWS), 0)
    rows = rows.astype(f32)
    for group in range(lse.shape[0]):
        for index, term in enumerate(three_terms(lse[group : group + 1, :])):
            rows = jnp.where(row == 3 + 3 * group + index, term, rows)
    return rows.astype(bf16)


def arrange_kernel(moved_ref, lse_ref, slots_ref):
    for owner in range(2):
        lse = lse_ref[HALF * owner : HALF * (owner + 1), :]
        for slot in range(SPAN):
            slots_ref[slot, owner, 0:512, :] = moved_ref[owner, slot, 0:512, :]
            slots_ref[slot, owner, 512:528, :] = with_lse(moved_ref[owner, slot, 512:528, :], lse)


def split_kernel(
    where_ref,
    table_ref,
    slots_ref,
    lse_ref,
    query_side_ref,
    key_side_ref,
    first_ref,
    second_ref,
    run_lse_ref,
):
    role, level = where_ref[0], where_ref[2]
    for slot in range(SPAN):
        for owner in range(2):
            block = 2 * table_ref[12 + slot] + owner
            query_side_ref[block, 0:256, :] = slots_ref[slot, owner, 0:256, :]
            key_side_ref[block, 0:256, :] = slots_ref[slot, owner, 256:512, :]
            rows = slots_ref[slot, owner, 512:528, :]
            at = 2 * slot + owner
            query_side_ref[block, 256:272, :] = with_lse(rows, lse_ref[at : at + 1, :])
            key_side_ref[block, 256:272, :] = jnp.zeros_like(rows)
            rows = rows.astype(f32)
            for group in range(HALF):
                first = 3 + 3 * group
                total = rows[first : first + 1] + rows[first + 1 : first + 2]
                run_lse_ref[slot, pl.ds(HALF * owner + group, 1), :] = (
                    total + rows[first + 2 : first + 3]
                )

    @pl.when(role == 0)
    def _():
        first_ref[...] = key_side_ref[...]

    @pl.when(role != 0)
    def _():
        first_ref[...] = query_side_ref[...]

    @pl.when((role == 0) | (level > 1))
    def _():
        second_ref[...] = query_side_ref[...]

    @pl.when((role != 0) & (level < 2))
    def _():
        second_ref[...] = key_side_ref[...]


def lse_kernel(where_ref, table_ref, run_lse_ref, *rest):
    shifted_refs, given_ref = rest[:-1], rest[-1]
    place, level = where_ref[1], where_ref[2]
    shift = lax.rem(level - place + SPAN, SPAN)

    def fill(source_ref):
        for index, height in enumerate((level, level ^ 1, 3 - level)):
            for run in range(SPAN):
                rank = rank_at(height, table_ref[16 + run])
                rows = source_ref[run, pl.ds(2 * height, 2), :]
                given_ref[index, pl.ds(2 * rank, 2), :] = rows

    for index, source_ref in enumerate((run_lse_ref, *shifted_refs)):

        @pl.when(shift == index)
        def _():
            fill(source_ref)


def read_rows(query_side_ref, lse_ref, delta_ref, given=None):
    for block in range(OWNERS):
        rows = query_side_ref[block, 256:272, :].astype(f32)
        half, part = block // HALF, block % HALF
        columns = slice(part * ROWS, (part + 1) * ROWS)
        delta_ref[half, :, columns] = rows[0:1] + rows[1:2] + rows[2:3]
        lse = rows[3:4] + rows[4:5] + rows[5:6]
        if given is not None:
            given_ref, index = given
            lse = given_ref[index, block : block + 1, :]
        lse_ref[half, :, columns] = lse * LOG2E


def nt(left, right):
    return lax.dot_general(left, right, (((1,), (1,)), ((), ())), preferred_element_type=f32)


def nn(left, right):
    return lax.dot_general(left, right, (((1,), (0,)), ((), ())), preferred_element_type=f32)


def tn(left, right):
    return lax.dot_general(left, right, (((0,), (0,)), ((), ())), preferred_element_type=f32)


def block_grads(query_half, key_half, query_refs, key_refs, chunks):
    query_side_ref, lse_ref, delta_ref, grad_query_ref = query_refs
    key_side_ref, grad_key_ref, grad_value_ref = key_refs
    size = HALF * ROWS
    keys_at = pl.ds(key_half * HALF, HALF)
    queries_at = pl.ds(query_half * HALF, HALF)
    key = key_side_ref[keys_at, 0:128, :].reshape(size, HEAD_DIM)
    value = key_side_ref[keys_at, 128:256, :].reshape(size, HEAD_DIM)
    query = query_side_ref[queries_at, 0:128, :].reshape(size, HEAD_DIM)
    cotangent = query_side_ref[queries_at, 128:256, :].reshape(size, HEAD_DIM)
    scores = nt(key, query)
    probs = jnp.exp2(scores * (SCALE * LOG2E) - lse_ref[query_half])
    if chunks is not None:
        (query_low, query_high), (key_low, key_high) = chunks
        at_query = lax.broadcasted_iota(jnp.int32, (1, size), 1)
        at_key = lax.broadcasted_iota(jnp.int32, (size, 1), 0)
        at_query += jnp.where(at_query < CHUNK, query_low * CHUNK, query_high * CHUNK - CHUNK)
        at_key += jnp.where(at_key < CHUNK, key_low * CHUNK, key_high * CHUNK - CHUNK)
        probs = jnp.where(at_query >= at_key, probs, 0.0)
    grad_probs = nt(value, cotangent)
    grad_scores = (probs * (grad_probs - delta_ref[query_half])).astype(bf16)
    shape = (HALF, ROWS, HEAD_DIM)
    grad_value_ref[keys_at] += nn(probs.astype(bf16), cotangent).reshape(shape)
    grad_key_ref[keys_at] += nn(grad_scores, query).reshape(shape)
    grad_query_ref[queries_at] += tn(grad_scores, key).reshape(shape)


def stairs_grads(table_ref, query_side, key_side, query_refs, key_refs):
    def chunks(half):
        at_query, at_key = 4 * query_side + 2 * half, 4 * key_side + 2 * half
        return (
            (table_ref[at_query], table_ref[at_query + 1]),
            (table_ref[at_key], table_ref[at_key + 1]),
        )

    block_grads(1, 0, query_refs, key_refs, None)
    block_grads(0, 0, query_refs, key_refs, chunks(0))
    block_grads(1, 1, query_refs, key_refs, chunks(1))


def paired_grads(table_ref, query_side, key_side, query_refs, key_refs):
    half = jnp.where(table_ref[4 * query_side] < table_ref[4 * key_side], 1, 0)
    block_grads(1, 0, query_refs, key_refs, None)
    block_grads(half, half, query_refs, key_refs, None)


def whole_grads(query_refs, key_refs):
    for query_half in range(2):
        for key_half in range(2):
            block_grads(query_half, key_half, query_refs, key_refs, None)


def own_kernel(
    where_ref,
    table_ref,
    query_side_ref,
    key_side_ref,
    given_ref,
    last_query_ref,
    last_key_ref,
    last_value_ref,
    grad_query_ref,
    grad_key_ref,
    grad_value_ref,
    *rows,
):
    grad_query_ref[...] = last_query_ref[...]
    grad_key_ref[...] = last_key_ref[...]
    grad_value_ref[...] = last_value_ref[...]

    @pl.when(where_ref[0] == 0)
    def _():
        read_rows(query_side_ref, *rows)

    @pl.when(where_ref[0] != 0)
    def _():
        read_rows(query_side_ref, *rows, (given_ref, 0))

    query_refs = (query_side_ref, *rows, grad_query_ref)
    stairs_grads(table_ref, 0, 0, query_refs, (key_side_ref, grad_key_ref, grad_value_ref))


def first_kernel(
    where_ref,
    table_ref,
    query_side_ref,
    key_side_ref,
    first_ref,
    given_ref,
    grad_query_ref,
    grad_key_ref,
    grad_value_ref,
    first_sum_ref,
    first_value_ref,
    *rows,
):
    for ref in (grad_query_ref, grad_key_ref, grad_value_ref, first_sum_ref, first_value_ref):
        ref[...] = jnp.zeros_like(ref)

    @pl.when(where_ref[0] == 0)
    def _():
        read_rows(query_side_ref, *rows)
        query_refs = (query_side_ref, *rows, grad_query_ref)
        paired_grads(table_ref, 0, 1, query_refs, (first_ref, first_sum_ref, first_value_ref))

    @pl.when(where_ref[0] != 0)
    def _():
        read_rows(first_ref, *rows, (given_ref, 1))
        query_refs = (first_ref, *rows, first_sum_ref)
        stairs_grads(table_ref, 1, 0, query_refs, (key_side_ref, grad_key_ref, grad_value_ref))


def second_kernel(
    where_ref,
    table_ref,
    key_side_ref,
    first_ref,
    second_ref,
    given_ref,
    last_key_ref,
    last_value_ref,
    last_sum_ref,
    last_far_value_ref,
    grad_key_ref,
    grad_value_ref,
    query_sum_ref,
    late_back_ref,
    key_back_ref,
    key_sum,
    value_sum,
    *rows,
):
    role, level = where_ref[0], where_ref[2]
    grad_key_ref[...] = last_key_ref[...]
    grad_value_ref[...] = last_value_ref[...]

    @pl.when(role == 0)
    def _():
        key_sum[...] = last_sum_ref[...]
        value_sum[...] = last_far_value_ref[...]
        query_sum_ref[...] = jnp.zeros_like(query_sum_ref)
        read_rows(second_ref, *rows)
        query_refs = (second_ref, *rows, query_sum_ref)
        paired_grads(table_ref, 2, 1, query_refs, (first_ref, key_sum, value_sum))

    @pl.when(role != 0)
    def _():
        query_sum_ref[...] = last_sum_ref[...]
        key_sum[...] = jnp.zeros_like(key_sum)
        value_sum[...] = jnp.zeros_like(value_sum)

    @pl.when((role != 0) & (level < 2))
    def _():
        read_rows(second_ref, *rows, (given_ref, 2))
        query_refs = (second_ref, *rows, key_sum)
        whole_grads(query_refs, (key_side_ref, grad_key_ref, grad_value_ref))
        late_back_ref[...] = (key_sum[...] * SCALE).astype(bf16)

    @pl.when((role != 0) & (level > 1))
    def _():
        read_rows(first_ref, *rows, (given_ref, 1))
        query_refs = (first_ref, *rows, query_sum_ref)
        whole_grads(query_refs, (second_ref, key_sum, value_sum))

    @pl.when((role == 0) | (level > 1))
    def _():
        key_back_ref[0] = (key_sum[...] * SCALE).astype(bf16)
        key_back_ref[1] = value_sum[...].astype(bf16)


def third_kernel(
    where_ref,
    table_ref,
    key_side_ref,
    second_ref,
    last_key_ref,
    last_value_ref,
    last_sum_ref,
    grad_key_ref,
    grad_value_ref,
    query_back_ref,
    query_sum,
    *rows,
):
    grad_key_ref[...] = last_key_ref[...]
    grad_value_ref[...] = last_value_ref[...]
    query_sum[...] = last_sum_ref[...]

    @pl.when(where_ref[0] == 0)
    def _():
        read_rows(second_ref, *rows)
        query_refs = (second_ref, *rows, query_sum)
        paired_grads(table_ref, 2, 0, query_refs, (key_side_ref, grad_key_ref, grad_value_ref))

    query_back_ref[...] = (query_sum[...] * SCALE).astype(bf16)


def join_kernel(
    table_ref,
    grad_query_ref,
    grad_key_ref,
    grad_value_ref,
    query_back_ref,
    late_back_ref,
    key_back_ref,
    slots_ref,
):
    for slot in range(SPAN):
        for owner in range(2):
            at = 2 * table_ref[12 + slot] + owner
            back = query_back_ref[at].astype(f32) + late_back_ref[at].astype(f32)
            sums = (
                grad_query_ref[at] * SCALE + back,
                grad_key_ref[at] * SCALE + key_back_ref[0, at].astype(f32),
                grad_value_ref[at] + key_back_ref[1, at].astype(f32),
            )
            for index, total in enumerate(sums):
                slots_ref[slot, owner, index * ROWS : (index + 1) * ROWS, :] = total.astype(bf16)


def turn_kernel(slots_ref, owners_ref):
    for owner in range(2):
        for slot in range(SPAN):
            owners_ref[owner, slot] = slots_ref[slot, owner]


def unpack_kernel(moved_ref, grad_query_ref, grad_key_ref, grad_value_ref, sent):
    moves = []
    for head in range(HEADS):
        columns = pl.ds(head * HEAD_DIM, HEAD_DIM)
        for index, target in enumerate((grad_query_ref, grad_key_ref, grad_value_ref)):
            source = moved_ref.at[head % 2, head // 2, pl.ds(index * ROWS, ROWS), :]
            moves.append(
                pltpu.make_async_copy(source, target.at[:, columns], sent.at[index, head])
            )
    for move in moves:
        move.start()
    for move in moves:
        move.wait()


def call(kernel, args, specs, outs, scratch=(), flops=0, moved=4 << 20, name=None, spaces=None):
    return pl.pallas_call(
        kernel,
        out_shape=[jax.ShapeDtypeStruct(shape, dtype) for shape, dtype in outs],
        in_specs=specs,
        out_specs=[VMEM] * len(outs) if spaces is None else spaces,
        scratch_shapes=list(scratch),
        compiler_params=PARAMS,
        cost_estimate=pl.CostEstimate(flops=flops, bytes_accessed=moved, transcendentals=0),
        name=name,
    )(*args)


def passed_along(value, axis, steps):
    count = lax.axis_size(axis)
    pairs = [(source, (source + steps) % count) for source in range(count)]
    return lax.ppermute(value, axis, pairs)


def block_length(row_total):
    length = row_total
    while length > 512 and length % 2 == 0:
        length = length // 2
    return length


def tile_grads(
    query_tile, cotangent_tile, lse_tile, delta_tile, query_place, key_tile, value_tile, key_place
):
    scaling = query_tile.shape[-1] ** (-0.5)
    scores = (
        jnp.einsum("qhd,khd->hqk", query_tile, key_tile, preferred_element_type=jnp.float32)
        * scaling
    )
    visible = query_place[:, None] >= key_place[None, :]
    probs = jnp.where(visible[None], jnp.exp(scores - lse_tile.T[:, :, None]), jnp.float32(0.0))
    probs_low = probs.astype(jnp.bfloat16)
    grad_probs = jnp.einsum(
        "qhd,khd->hqk", cotangent_tile, value_tile, preferred_element_type=jnp.float32
    )
    grad_scores = (probs * (grad_probs - delta_tile.T[:, :, None])).astype(jnp.bfloat16)
    grad_query = (
        jnp.einsum("hqk,khd->qhd", grad_scores, key_tile, preferred_element_type=jnp.float32)
        * scaling
    )
    grad_key = (
        jnp.einsum("hqk,qhd->khd", grad_scores, query_tile, preferred_element_type=jnp.float32)
        * scaling
    )
    grad_value = jnp.einsum(
        "hqk,qhd->khd", probs_low, cotangent_tile, preferred_element_type=jnp.float32
    )
    return (grad_query, grad_key, grad_value)


def visit(
    query_tile, cotangent_tile, lse_tile, delta_tile, query_place, key_tile, value_tile, key_place
):
    key_count, heads_dev, head_dim = key_tile.shape
    length = block_length(key_count)
    block_total = key_count // length

    def key_step(running, tiles):
        key_part, value_part, place_part = tiles
        grads = tile_grads(
            query_tile,
            cotangent_tile,
            lse_tile,
            delta_tile,
            query_place,
            key_part,
            value_part,
            place_part,
        )
        return (running + grads[0], (grads[1], grads[2]))

    start_query = jnp.zeros(query_tile.shape, jnp.float32)
    grad_query, (grad_key, grad_value) = lax.scan(
        key_step,
        start_query,
        (
            key_tile.reshape(block_total, length, heads_dev, head_dim),
            value_tile.reshape(block_total, length, heads_dev, head_dim),
            key_place.reshape(block_total, length),
        ),
    )
    return (
        grad_query,
        grad_key.reshape(key_count, heads_dev, head_dim),
        grad_value.reshape(key_count, heads_dev, head_dim),
    )


def any_order(queries, key_rows, value_rows, attn_output, grad_output, logsumexp, positions):
    heads_dev = logsumexp.shape[1]
    moved = (
        lax.all_to_all(queries, "ulysses", split_axis=1, concat_axis=0, tiled=True),
        lax.all_to_all(key_rows, "ulysses", split_axis=1, concat_axis=0, tiled=True),
        lax.all_to_all(value_rows, "ulysses", split_axis=1, concat_axis=0, tiled=True),
        lax.all_to_all(attn_output, "ulysses", split_axis=1, concat_axis=0, tiled=True),
        lax.all_to_all(grad_output, "ulysses", split_axis=1, concat_axis=0, tiled=True),
    )
    row_count = moved[0].shape[0]
    head_dim = moved[0].shape[1] // heads_dev
    query_heads = moved[0].reshape(row_count, heads_dev, head_dim)
    key_heads = moved[1].reshape(row_count, heads_dev, head_dim)
    value_heads = moved[2].reshape(row_count, heads_dev, head_dim)
    output_heads = moved[3].reshape(row_count, heads_dev, head_dim)
    cotangent_heads = moved[4].reshape(row_count, heads_dev, head_dim)
    delta_own = jnp.sum(
        cotangent_heads.astype(jnp.float32) * output_heads.astype(jnp.float32), axis=-1
    )
    blk_count = lax.axis_size("blk")
    stride = blk_count // SPAN
    blk_place = lax.axis_index("blk")

    def rows_of(holder):
        return lax.dynamic_slice_in_dim(positions, holder * row_count, row_count)

    own_place = rows_of(blk_place)
    zeros_grad = jnp.zeros((row_count, heads_dev, head_dim), jnp.float32)
    visiting = (query_heads, cotangent_heads)
    carried = (zeros_grad, logsumexp, delta_own)
    grad_key = zeros_grad
    grad_value = zeros_grad
    for turn in range(SPAN):
        holder = (blk_place - turn * stride) % blk_count
        grads = visit(
            visiting[0],
            visiting[1],
            carried[1],
            carried[2],
            rows_of(holder),
            key_heads,
            value_heads,
            own_place,
        )
        grad_key = grad_key + grads[1]
        grad_value = grad_value + grads[2]
        if turn + 1 < SPAN:
            visiting = passed_along((visiting[0], visiting[1]), "blk", stride)
        carried = passed_along((carried[0] + grads[0], carried[1], carried[2]), "blk", stride)
    grad_query = carried[0]
    width = heads_dev * head_dim
    low_query = grad_query.astype(jnp.bfloat16).reshape(row_count, width)
    low_key = grad_key.astype(jnp.bfloat16).reshape(row_count, width)
    low_value = grad_value.astype(jnp.bfloat16).reshape(row_count, width)
    back = (
        lax.all_to_all(low_query, "ulysses", split_axis=0, concat_axis=1, tiled=True),
        lax.all_to_all(low_key, "ulysses", split_axis=0, concat_axis=1, tiled=True),
        lax.all_to_all(low_value, "ulysses", split_axis=0, concat_axis=1, tiled=True),
    )
    return (back[0], back[1], back[2])


def row_scratch():
    return pltpu.VMEM((2, 1, HALF * ROWS), f32)


def per_device(queries, key_rows, value_rows, attn_output, grad_output, logsumexp, positions):
    blk_count = lax.axis_size("blk")
    stride = blk_count // SPAN
    rank, here = lax.axis_index("ulysses"), lax.axis_index("blk")
    line = here % stride
    role = (rank % 2) ^ (2 * line // stride)
    where = jnp.stack([role, here // stride, rank // 2, line, jnp.int32(stride)])

    def index_of(role, place, level, at):
        core = role ^ (2 * at // stride)
        return (2 * level + core) * blk_count + place * stride + at

    spots = [(p, z, at) for p in range(SPAN) for z in range(SPAN) for at in range(stride)]

    def swapped(value, over_x, over_z, levels=range(SPAN)):
        pairs = []
        for p, z, at in spots:
            if over_x is not None:
                pairs.append((index_of(0, p, z, at), index_of(0, over_x(p), z, at)))
            if z in levels:
                pairs.append((index_of(1, p, z, at), index_of(1, p, over_z(z), at)))
        return lax.ppermute(value, AXES, pairs)

    mate = lambda at: at ^ 1
    mirror = lambda at: SPAN - 1 - at

    def level_shift(value, shift):
        pairs = [
            (index_of(1, p, p, at), index_of(1, p, (p + shift) % SPAN, at))
            for p in range(SPAN)
            for at in range(stride)
        ]
        return lax.ppermute(value, AXES, pairs)

    core_groups = [sorted(index_of(role, p, z, at) for role in range(2)) for p, z, at in spots]
    over_z = lambda role: [
        [index_of(role, p, z, at) for z in range(SPAN)] for p in range(SPAN) for at in range(stride)
    ]
    over_x = lambda role: [
        [index_of(role, p, z, at) for p in range(SPAN)] for z in range(SPAN) for at in range(stride)
    ]
    head_groups = over_z(0) + over_x(1)

    def exchanged(value, groups):
        return lax.all_to_all(
            value, AXES, split_axis=0, concat_axis=0, axis_index_groups=groups, tiled=True
        )

    side = (OWNERS, ROWS, HEAD_DIM)
    lse = logsumexp.reshape(OWNERS, ROWS)
    tokens = [
        pltpu.with_memory_space_constraint(value, pltpu.HBM)
        for value in (queries, key_rows, value_rows, attn_output, grad_output, positions)
    ]
    packed, table = call(
        pack_kernel,
        (where, *tokens),
        [SMEM] + [HBM] * 6,
        [((2, SPAN, PART, HEAD_DIM), bf16), ((20,), jnp.int32)],
        [
            pltpu.VMEM((HEADS, ROWS, HEAD_DIM), bf16),
            pltpu.SMEM((SPAN, 128), jnp.int32),
            pltpu.SemaphoreType.DMA((5, HEADS)),
            pltpu.SemaphoreType.DMA((SPAN,)),
        ],
        name="pack",
        spaces=[VMEM, SMEM],
    )
    (slots,) = call(
        arrange_kernel,
        (exchanged(packed, core_groups), lse),
        [VMEM] * 2,
        [((SPAN, 2, PART, HEAD_DIM), bf16)],
        name="arrange",
    )
    card = ((OWNERS, 272, HEAD_DIM), bf16)
    rows = [row_scratch(), row_scratch()]
    query_side, key_side, first_out, second_out, run_lse = call(
        split_kernel,
        (where, table, exchanged(slots, head_groups), lse),
        [SMEM] * 2 + [VMEM] * 2,
        [card] * 4 + [((SPAN, OWNERS, ROWS), f32)],
        name="split",
    )
    first = swapped(first_out, mirror, mate)
    second = swapped(second_out, mate, mirror)
    cost = 10 * 128 * 2 * 512 * 512
    (given,) = call(
        lse_kernel,
        (where, table, run_lse, *(level_shift(run_lse, shift) for shift in range(1, SPAN))),
        [SMEM] * 2 + [VMEM] * 4,
        [((3, OWNERS, ROWS), f32)],
        name="lse",
    )
    grad_query, grad_key, grad_value, first_sum, first_value = call(
        first_kernel,
        (where, table, query_side, key_side, first, given),
        [SMEM] * 2 + [VMEM] * 4,
        [(side, f32)] * 5,
        rows,
        flops=cost,
        name="first",
    )
    grad_key, grad_value, query_sum, late_back, key_back = call(
        second_kernel,
        (where, table, key_side, first, second, given, grad_key, grad_value, first_sum, first_value),
        [SMEM] * 2 + [VMEM] * 8,
        [(side, f32)] * 3 + [(side, bf16), ((2,) + side, bf16)],
        [pltpu.VMEM(side, f32), pltpu.VMEM(side, f32)] + rows,
        flops=cost,
        name="second",
    )
    key_back = swapped(key_back, mirror, mirror, (2, 3))
    grad_key, grad_value, query_back = call(
        third_kernel,
        (where, table, key_side, second, grad_key, grad_value, query_sum),
        [SMEM] * 2 + [VMEM] * 5,
        [(side, f32)] * 2 + [(side, bf16)],
        [pltpu.VMEM(side, f32)] + rows,
        flops=4 * cost,
        name="third",
    )
    query_back = swapped(query_back, mate, mate)
    late_back = swapped(late_back, None, mirror, (0, 1))
    grad_query, grad_key, grad_value = call(
        own_kernel,
        (where, table, query_side, key_side, given, grad_query, grad_key, grad_value),
        [SMEM] * 2 + [VMEM] * 6,
        [(side, f32)] * 3,
        rows,
        flops=1,
        moved=1,
        name="own",
    )
    (joined,) = call(
        join_kernel,
        (table, grad_query, grad_key, grad_value, query_back, late_back, key_back),
        [SMEM] + [VMEM] * 6,
        [((SPAN, 2, 3 * ROWS, HEAD_DIM), bf16)],
        name="join",
    )
    (turned,) = call(
        turn_kernel,
        (exchanged(joined, head_groups),),
        [VMEM],
        [((2, SPAN, 3 * ROWS, HEAD_DIM), bf16)],
        name="turn",
    )
    returned = exchanged(turned, core_groups)

    def rising():
        return tuple(
            call(
                unpack_kernel,
                (returned,),
                [VMEM],
                [((ROWS, HEADS * HEAD_DIM), bf16)] * 3,
                [pltpu.SemaphoreType.DMA((3, HEADS))],
                name="unpack",
                spaces=[HBM] * 3,
            )
        )

    def falling():
        return any_order(
            queries, key_rows, value_rows, attn_output, grad_output, logsumexp, positions
        )

    first_places = lax.slice(positions, (0,), positions.shape, (OWNERS * ROWS,))
    return lax.cond(jnp.any(first_places >= SPAN * 2 * CHUNK), falling, rising)


def solution(mesh):
    tokens = P(("blk", "ulysses"), None)
    return jax.shard_map(
        per_device,
        mesh=mesh,
        in_specs=(tokens,) * 5 + (P("blk", "ulysses"), P()),
        out_specs=(tokens,) * 3,
        check_vma=False,
    )
```

```python
import jax
import jax.numpy as jnp
from jax import lax
from jax.experimental import pallas as pl
from jax.experimental.pallas import tpu as pltpu
from jax.sharding import PartitionSpec as P

SPAN = 4
HEAD_DIM = 128
LOG2E = 1.4426950408889634
SCALE = HEAD_DIM ** -0.5
ROWS = 128
HEADS = 8
OWNERS = 8
HALF = 4
CHUNK = 256
EXTRA = 16
PART = 4 * ROWS + EXTRA
AXES = ("ulysses", "blk")
f32 = jnp.float32
bf16 = jnp.bfloat16
VMEM = pl.BlockSpec(memory_space=pltpu.VMEM)
SMEM = pl.BlockSpec(memory_space=pltpu.SMEM)
HBM = pl.BlockSpec(memory_space=pltpu.HBM)
PARAMS = pltpu.CompilerParams(vmem_limit_bytes=24 * 1024 * 1024)


def three_terms(row):
    high = row.astype(bf16).astype(f32)
    rest = row - high
    middle = rest.astype(bf16).astype(f32)
    return (high, middle, rest - middle)


def chunk_at(level, pair):
    return jnp.where(
        level == 0,
        2 * pair,
        jnp.where(level == 1, 2 * pair + 1, jnp.where(level == 2, 14 - 2 * pair, 15 - 2 * pair)),
    )


def rank_at(level, pair):
    return jnp.where(level < 2, pair, 3 - pair)


def fill_table(table_ref, pairs, role, place, level):
    def pick(at):
        value = pairs[0]
        for index in range(1, SPAN):
            value = jnp.where(at == index, pairs[index], value)
        return value

    sides = ((place, level), (SPAN - 1 - place, level ^ 1), (place ^ 1, 3 - level))
    for side, (run, height) in enumerate(sides):
        pair = pick(run)
        for index in range(4):
            over_x = chunk_at(jnp.int32(index), pair)
            over_z = 2 * index + jnp.where(height < 2, height, height + 6)
            table_ref[4 * side + index] = jnp.where(role == 0, over_x, over_z)
    for slot in range(SPAN):
        table_ref[12 + slot] = jnp.where(role == 0, slot, rank_at(level, pairs[slot]))
        table_ref[16 + slot] = pairs[slot]
    for index, value in enumerate((role, place, level)):
        table_ref[20 + index] = value


def pack_kernel(
    query_ref,
    key_ref,
    value_ref,
    output_ref,
    cotangent_ref,
    positions_ref,
    packed_ref,
    table_ref,
    output_here,
    places,
    arrived,
    places_arrived,
):
    stride = lax.axis_size("blk") // SPAN
    rank, here = lax.axis_index("ulysses"), lax.axis_index("blk")
    place, line, level = lax.div(here, stride), lax.rem(here, stride), lax.div(rank, 2)
    role = lax.rem(rank, 2) ^ lax.div(2 * line, stride)
    run_rows = OWNERS * ROWS
    first_places = []
    for run in range(SPAN):
        start = pl.multiple_of((run * stride + line) * run_rows, run_rows)
        first_places.append(
            pltpu.make_async_copy(
                positions_ref.at[pl.ds(start, 128)], places.at[run], places_arrived.at[run]
            )
        )

    def copies(index, source):
        for head in range(HEADS):
            columns = pl.ds(head * HEAD_DIM, HEAD_DIM)
            target = output_here.at[head]
            if index < 4:
                target = packed_ref.at[head % 2, head // 2, pl.ds(index * ROWS, ROWS), :]
            yield pltpu.make_async_copy(source.at[:, columns], target, arrived.at[index, head])

    sources = (query_ref, cotangent_ref, key_ref, value_ref, output_ref)
    moves = [list(copies(index, source)) for index, source in enumerate(sources)]
    for move in first_places:
        move.start()
    for index in (1, 4, 0, 2, 3):
        for move in moves[index]:
            move.start()
    for move in first_places:
        move.wait()
    pairs = [
        jnp.minimum(lax.div(places[run, 0], jnp.int32(2 * CHUNK)), SPAN - 1) for run in range(SPAN)
    ]
    fill_table(table_ref, pairs, role, place, level)
    row = lax.broadcasted_iota(jnp.int32, (EXTRA, ROWS), 0)
    for head in range(HEADS):
        moves[1][head].wait()
        moves[4][head].wait()
        cotangent = packed_ref[head % 2, head // 2, 128:256, :].astype(f32)
        delta = jnp.sum((cotangent * output_here[head].astype(f32)).T, axis=0, keepdims=True)
        high, middle, low = three_terms(delta)
        rows = jnp.where(row == 0, high, jnp.where(row == 1, middle, jnp.where(row == 2, low, 0.0)))
        packed_ref[head % 2, head // 2, 512:528, :] = rows.astype(bf16)
    for index in (0, 2, 3):
        for move in moves[index]:
            move.wait()


def with_lse(rows, lse):
    row = lax.broadcasted_iota(jnp.int32, (EXTRA, ROWS), 0)
    rows = rows.astype(f32)
    for group in range(lse.shape[0]):
        for index, term in enumerate(three_terms(lse[group : group + 1, :])):
            rows = jnp.where(row == 3 + 3 * group + index, term, rows)
    return rows.astype(bf16)


def arrange_kernel(moved_ref, lse_ref, slots_ref):
    for owner in range(2):
        lse = lse_ref[HALF * owner : HALF * (owner + 1), :]
        for slot in range(SPAN):
            slots_ref[slot, owner, 0:512, :] = moved_ref[owner, slot, 0:512, :]
            slots_ref[slot, owner, 512:528, :] = with_lse(moved_ref[owner, slot, 512:528, :], lse)


def split_kernel(
    table_ref,
    slots_ref,
    lse_ref,
    query_side_ref,
    key_side_ref,
    first_ref,
    second_ref,
    run_lse_ref,
):
    role, level = table_ref[20], table_ref[22]
    for slot in range(SPAN):
        for owner in range(2):
            block = 2 * table_ref[12 + slot] + owner
            query_side_ref[block, 0:256, :] = slots_ref[slot, owner, 0:256, :]
            key_side_ref[block, 0:256, :] = slots_ref[slot, owner, 256:512, :]
            rows = slots_ref[slot, owner, 512:528, :]
            at = 2 * slot + owner
            query_side_ref[block, 256:272, :] = with_lse(rows, lse_ref[at : at + 1, :])
            key_side_ref[block, 256:272, :] = jnp.zeros_like(rows)
            rows = rows.astype(f32)
            for group in range(HALF):
                first = 3 + 3 * group
                total = rows[first : first + 1] + rows[first + 1 : first + 2]
                run_lse_ref[slot, pl.ds(HALF * owner + group, 1), :] = (
                    total + rows[first + 2 : first + 3]
                )

    @pl.when(role == 0)
    def _():
        first_ref[...] = key_side_ref[...]

    @pl.when(role != 0)
    def _():
        first_ref[...] = query_side_ref[...]

    @pl.when((role == 0) | (level > 1))
    def _():
        second_ref[...] = query_side_ref[...]

    @pl.when((role != 0) & (level < 2))
    def _():
        second_ref[...] = key_side_ref[...]


def lse_kernel(table_ref, run_lse_ref, *rest):
    shifted_refs, given_ref = rest[:-1], rest[-1]
    place, level = table_ref[21], table_ref[22]
    shift = lax.rem(level - place + SPAN, SPAN)

    def fill(source_ref):
        for index, height in enumerate((level, level ^ 1, 3 - level)):
            for run in range(SPAN):
                rank = rank_at(height, table_ref[16 + run])
                rows = source_ref[run, pl.ds(2 * height, 2), :]
                given_ref[index, pl.ds(2 * rank, 2), :] = rows

    for index, source_ref in enumerate((run_lse_ref, *shifted_refs)):

        @pl.when(shift == index)
        def _():
            fill(source_ref)


def read_rows(query_side_ref, lse_ref, delta_ref, given=None):
    for block in range(OWNERS):
        rows = query_side_ref[block, 256:272, :].astype(f32)
        half, part = block // HALF, block % HALF
        columns = slice(part * ROWS, (part + 1) * ROWS)
        delta_ref[half, :, columns] = rows[0:1] + rows[1:2] + rows[2:3]
        lse = rows[3:4] + rows[4:5] + rows[5:6]
        if given is not None:
            given_ref, index = given
            lse = given_ref[index, block : block + 1, :]
        lse_ref[half, :, columns] = lse * LOG2E


def nt(left, right):
    return lax.dot_general(left, right, (((1,), (1,)), ((), ())), preferred_element_type=f32)


def nn(left, right):
    return lax.dot_general(left, right, (((1,), (0,)), ((), ())), preferred_element_type=f32)


def tn(left, right):
    return lax.dot_general(left, right, (((0,), (0,)), ((), ())), preferred_element_type=f32)


def block_grads(query_half, key_half, query_refs, key_refs, chunks):
    query_side_ref, lse_ref, delta_ref, grad_query_ref = query_refs
    key_side_ref, grad_key_ref, grad_value_ref = key_refs
    size = HALF * ROWS
    keys_at = pl.ds(key_half * HALF, HALF)
    queries_at = pl.ds(query_half * HALF, HALF)
    key = key_side_ref[keys_at, 0:128, :].reshape(size, HEAD_DIM)
    value = key_side_ref[keys_at, 128:256, :].reshape(size, HEAD_DIM)
    query = query_side_ref[queries_at, 0:128, :].reshape(size, HEAD_DIM)
    cotangent = query_side_ref[queries_at, 128:256, :].reshape(size, HEAD_DIM)
    scores = nt(key, query)
    probs = jnp.exp2(scores * (SCALE * LOG2E) - lse_ref[query_half])
    if chunks is not None:
        (query_low, query_high), (key_low, key_high) = chunks
        at_query = lax.broadcasted_iota(jnp.int32, (1, size), 1)
        at_key = lax.broadcasted_iota(jnp.int32, (size, 1), 0)
        at_query += jnp.where(at_query < CHUNK, query_low * CHUNK, query_high * CHUNK - CHUNK)
        at_key += jnp.where(at_key < CHUNK, key_low * CHUNK, key_high * CHUNK - CHUNK)
        probs = jnp.where(at_query >= at_key, probs, 0.0)
    grad_probs = nt(value, cotangent)
    grad_scores = (probs * (grad_probs - delta_ref[query_half])).astype(bf16)
    shape = (HALF, ROWS, HEAD_DIM)
    grad_value_ref[keys_at] += nn(probs.astype(bf16), cotangent).reshape(shape)
    grad_key_ref[keys_at] += nn(grad_scores, query).reshape(shape)
    grad_query_ref[queries_at] += tn(grad_scores, key).reshape(shape)


def stairs_grads(table_ref, query_side, key_side, query_refs, key_refs):
    def chunks(half):
        at_query, at_key = 4 * query_side + 2 * half, 4 * key_side + 2 * half
        return (
            (table_ref[at_query], table_ref[at_query + 1]),
            (table_ref[at_key], table_ref[at_key + 1]),
        )

    block_grads(1, 0, query_refs, key_refs, None)
    block_grads(0, 0, query_refs, key_refs, chunks(0))
    block_grads(1, 1, query_refs, key_refs, chunks(1))


def paired_grads(table_ref, query_side, key_side, query_refs, key_refs):
    half = jnp.where(table_ref[4 * query_side] < table_ref[4 * key_side], 1, 0)
    block_grads(1, 0, query_refs, key_refs, None)
    block_grads(half, half, query_refs, key_refs, None)


def whole_grads(query_refs, key_refs):
    for query_half in range(2):
        for key_half in range(2):
            block_grads(query_half, key_half, query_refs, key_refs, None)


def own_kernel(
    table_ref,
    _,
    query_side_ref,
    key_side_ref,
    given_ref,
    last_query_ref,
    last_key_ref,
    last_value_ref,
    grad_query_ref,
    grad_key_ref,
    grad_value_ref,
    *rows,
):
    grad_query_ref[...] = last_query_ref[...]
    grad_key_ref[...] = last_key_ref[...]
    grad_value_ref[...] = last_value_ref[...]

    @pl.when(table_ref[20] == 0)
    def _():
        read_rows(query_side_ref, *rows)

    @pl.when(table_ref[20] != 0)
    def _():
        read_rows(query_side_ref, *rows, (given_ref, 0))

    query_refs = (query_side_ref, *rows, grad_query_ref)
    stairs_grads(table_ref, 0, 0, query_refs, (key_side_ref, grad_key_ref, grad_value_ref))


def first_kernel(
    table_ref,
    query_side_ref,
    key_side_ref,
    first_ref,
    given_ref,
    grad_query_ref,
    grad_key_ref,
    grad_value_ref,
    first_sum_ref,
    first_value_ref,
    *rows,
):
    for ref in (grad_query_ref, grad_key_ref, grad_value_ref, first_sum_ref, first_value_ref):
        ref[...] = jnp.zeros_like(ref)

    @pl.when(table_ref[20] == 0)
    def _():
        read_rows(query_side_ref, *rows)
        query_refs = (query_side_ref, *rows, grad_query_ref)
        paired_grads(table_ref, 0, 1, query_refs, (first_ref, first_sum_ref, first_value_ref))

    @pl.when(table_ref[20] != 0)
    def _():
        read_rows(first_ref, *rows, (given_ref, 1))
        query_refs = (first_ref, *rows, first_sum_ref)
        stairs_grads(table_ref, 1, 0, query_refs, (key_side_ref, grad_key_ref, grad_value_ref))


def second_kernel(
    table_ref,
    key_side_ref,
    first_ref,
    second_ref,
    given_ref,
    last_key_ref,
    last_value_ref,
    last_sum_ref,
    last_far_value_ref,
    grad_key_ref,
    grad_value_ref,
    query_sum_ref,
    far_back_ref,
    key_sum,
    value_sum,
    *rows,
):
    role, level = table_ref[20], table_ref[22]
    grad_key_ref[...] = last_key_ref[...]
    grad_value_ref[...] = last_value_ref[...]

    @pl.when(role == 0)
    def _():
        key_sum[...] = last_sum_ref[...]
        value_sum[...] = last_far_value_ref[...]
        query_sum_ref[...] = jnp.zeros_like(query_sum_ref)
        read_rows(second_ref, *rows)
        query_refs = (second_ref, *rows, query_sum_ref)
        paired_grads(table_ref, 2, 1, query_refs, (first_ref, key_sum, value_sum))

    @pl.when(role != 0)
    def _():
        query_sum_ref[...] = last_sum_ref[...]
        key_sum[...] = jnp.zeros_like(key_sum)
        value_sum[...] = jnp.zeros_like(value_sum)

    @pl.when((role != 0) & (level < 2))
    def _():
        read_rows(second_ref, *rows, (given_ref, 2))
        query_refs = (second_ref, *rows, key_sum)
        whole_grads(query_refs, (key_side_ref, grad_key_ref, grad_value_ref))
        total = key_sum[...] * SCALE
        high = total.astype(bf16)
        far_back_ref[0] = high
        far_back_ref[1] = (total - high.astype(f32)).astype(bf16)

    @pl.when((role != 0) & (level > 1))
    def _():
        read_rows(first_ref, *rows, (given_ref, 1))
        query_refs = (first_ref, *rows, query_sum_ref)
        whole_grads(query_refs, (second_ref, key_sum, value_sum))

    @pl.when((role == 0) | (level > 1))
    def _():
        far_back_ref[0] = (key_sum[...] * SCALE).astype(bf16)
        far_back_ref[1] = value_sum[...].astype(bf16)


def third_kernel(
    table_ref,
    key_side_ref,
    second_ref,
    last_key_ref,
    last_value_ref,
    last_sum_ref,
    grad_key_ref,
    grad_value_ref,
    query_back_ref,
    query_sum,
    *rows,
):
    grad_key_ref[...] = last_key_ref[...]
    grad_value_ref[...] = last_value_ref[...]
    query_sum[...] = last_sum_ref[...]

    @pl.when(table_ref[20] == 0)
    def _():
        read_rows(second_ref, *rows)
        query_refs = (second_ref, *rows, query_sum)
        paired_grads(table_ref, 2, 0, query_refs, (key_side_ref, grad_key_ref, grad_value_ref))

    query_back_ref[...] = (query_sum[...] * SCALE).astype(bf16)


def join_kernel(
    table_ref, grad_query_ref, grad_key_ref, grad_value_ref, query_back_ref, far_back_ref, slots_ref
):
    to_query = jnp.where((table_ref[20] != 0) & (table_ref[22] > 1), 1.0, 0.0).astype(f32)
    for slot in range(SPAN):
        for owner in range(2):
            at = 2 * table_ref[12 + slot] + owner
            back = query_back_ref[at].astype(f32)
            one, two = far_back_ref[0, at].astype(f32), far_back_ref[1, at].astype(f32)
            sums = (
                grad_query_ref[at] * SCALE + back + to_query * (one + two),
                grad_key_ref[at] * SCALE + (1.0 - to_query) * one,
                grad_value_ref[at] + (1.0 - to_query) * two,
            )
            for index, total in enumerate(sums):
                slots_ref[slot, owner, index * ROWS : (index + 1) * ROWS, :] = total.astype(bf16)


def turn_kernel(slots_ref, owners_ref):
    for owner in range(2):
        for slot in range(SPAN):
            owners_ref[owner, slot] = slots_ref[slot, owner]


def unpack_kernel(moved_ref, grad_query_ref, grad_key_ref, grad_value_ref, sent):
    moves = []
    for head in range(HEADS):
        columns = pl.ds(head * HEAD_DIM, HEAD_DIM)
        for index, target in enumerate((grad_query_ref, grad_key_ref, grad_value_ref)):
            source = moved_ref.at[head % 2, head // 2, pl.ds(index * ROWS, ROWS), :]
            moves.append(
                pltpu.make_async_copy(source, target.at[:, columns], sent.at[index, head])
            )
    for move in moves:
        move.start()
    for move in moves:
        move.wait()


def call(kernel, args, specs, outs, scratch=(), flops=0, moved=4 << 20, name=None, spaces=None):
    return pl.pallas_call(
        kernel,
        out_shape=[jax.ShapeDtypeStruct(shape, dtype) for shape, dtype in outs],
        in_specs=specs,
        out_specs=[VMEM] * len(outs) if spaces is None else spaces,
        scratch_shapes=list(scratch),
        compiler_params=PARAMS,
        cost_estimate=pl.CostEstimate(flops=flops, bytes_accessed=moved, transcendentals=0),
        name=name,
    )(*args)


def passed_along(value, axis, steps):
    count = lax.axis_size(axis)
    pairs = [(source, (source + steps) % count) for source in range(count)]
    return lax.ppermute(value, axis, pairs)


def block_length(row_total):
    length = row_total
    while length > 512 and length % 2 == 0:
        length = length // 2
    return length


def tile_grads(
    query_tile, cotangent_tile, lse_tile, delta_tile, query_place, key_tile, value_tile, key_place
):
    scaling = query_tile.shape[-1] ** (-0.5)
    scores = (
        jnp.einsum("qhd,khd->hqk", query_tile, key_tile, preferred_element_type=jnp.float32)
        * scaling
    )
    visible = query_place[:, None] >= key_place[None, :]
    probs = jnp.where(visible[None], jnp.exp(scores - lse_tile.T[:, :, None]), jnp.float32(0.0))
    probs_low = probs.astype(jnp.bfloat16)
    grad_probs = jnp.einsum(
        "qhd,khd->hqk", cotangent_tile, value_tile, preferred_element_type=jnp.float32
    )
    grad_scores = (probs * (grad_probs - delta_tile.T[:, :, None])).astype(jnp.bfloat16)
    grad_query = (
        jnp.einsum("hqk,khd->qhd", grad_scores, key_tile, preferred_element_type=jnp.float32)
        * scaling
    )
    grad_key = (
        jnp.einsum("hqk,qhd->khd", grad_scores, query_tile, preferred_element_type=jnp.float32)
        * scaling
    )
    grad_value = jnp.einsum(
        "hqk,qhd->khd", probs_low, cotangent_tile, preferred_element_type=jnp.float32
    )
    return (grad_query, grad_key, grad_value)


def visit(
    query_tile, cotangent_tile, lse_tile, delta_tile, query_place, key_tile, value_tile, key_place
):
    key_count, heads_dev, head_dim = key_tile.shape
    length = block_length(key_count)
    block_total = key_count // length

    def key_step(running, tiles):
        key_part, value_part, place_part = tiles
        grads = tile_grads(
            query_tile,
            cotangent_tile,
            lse_tile,
            delta_tile,
            query_place,
            key_part,
            value_part,
            place_part,
        )
        return (running + grads[0], (grads[1], grads[2]))

    start_query = jnp.zeros(query_tile.shape, jnp.float32)
    grad_query, (grad_key, grad_value) = lax.scan(
        key_step,
        start_query,
        (
            key_tile.reshape(block_total, length, heads_dev, head_dim),
            value_tile.reshape(block_total, length, heads_dev, head_dim),
            key_place.reshape(block_total, length),
        ),
    )
    return (
        grad_query,
        grad_key.reshape(key_count, heads_dev, head_dim),
        grad_value.reshape(key_count, heads_dev, head_dim),
    )


def any_order(queries, key_rows, value_rows, attn_output, grad_output, logsumexp, positions):
    heads_dev = logsumexp.shape[1]
    moved = (
        lax.all_to_all(queries, "ulysses", split_axis=1, concat_axis=0, tiled=True),
        lax.all_to_all(key_rows, "ulysses", split_axis=1, concat_axis=0, tiled=True),
        lax.all_to_all(value_rows, "ulysses", split_axis=1, concat_axis=0, tiled=True),
        lax.all_to_all(attn_output, "ulysses", split_axis=1, concat_axis=0, tiled=True),
        lax.all_to_all(grad_output, "ulysses", split_axis=1, concat_axis=0, tiled=True),
    )
    row_count = moved[0].shape[0]
    head_dim = moved[0].shape[1] // heads_dev
    query_heads = moved[0].reshape(row_count, heads_dev, head_dim)
    key_heads = moved[1].reshape(row_count, heads_dev, head_dim)
    value_heads = moved[2].reshape(row_count, heads_dev, head_dim)
    output_heads = moved[3].reshape(row_count, heads_dev, head_dim)
    cotangent_heads = moved[4].reshape(row_count, heads_dev, head_dim)
    delta_own = jnp.sum(
        cotangent_heads.astype(jnp.float32) * output_heads.astype(jnp.float32), axis=-1
    )
    blk_count = lax.axis_size("blk")
    stride = blk_count // SPAN
    blk_place = lax.axis_index("blk")

    def rows_of(holder):
        return lax.dynamic_slice_in_dim(positions, holder * row_count, row_count)

    own_place = rows_of(blk_place)
    zeros_grad = jnp.zeros((row_count, heads_dev, head_dim), jnp.float32)
    visiting = (query_heads, cotangent_heads)
    carried = (zeros_grad, logsumexp, delta_own)
    grad_key = zeros_grad
    grad_value = zeros_grad
    for turn in range(SPAN):
        holder = (blk_place - turn * stride) % blk_count
        grads = visit(
            visiting[0],
            visiting[1],
            carried[1],
            carried[2],
            rows_of(holder),
            key_heads,
            value_heads,
            own_place,
        )
        grad_key = grad_key + grads[1]
        grad_value = grad_value + grads[2]
        if turn + 1 < SPAN:
            visiting = passed_along((visiting[0], visiting[1]), "blk", stride)
        carried = passed_along((carried[0] + grads[0], carried[1], carried[2]), "blk", stride)
    grad_query = carried[0]
    width = heads_dev * head_dim
    low_query = grad_query.astype(jnp.bfloat16).reshape(row_count, width)
    low_key = grad_key.astype(jnp.bfloat16).reshape(row_count, width)
    low_value = grad_value.astype(jnp.bfloat16).reshape(row_count, width)
    back = (
        lax.all_to_all(low_query, "ulysses", split_axis=0, concat_axis=1, tiled=True),
        lax.all_to_all(low_key, "ulysses", split_axis=0, concat_axis=1, tiled=True),
        lax.all_to_all(low_value, "ulysses", split_axis=0, concat_axis=1, tiled=True),
    )
    return (back[0], back[1], back[2])


def row_scratch():
    return pltpu.VMEM((2, 1, HALF * ROWS), f32)


def per_device(queries, key_rows, value_rows, attn_output, grad_output, logsumexp, positions):
    blk_count = lax.axis_size("blk")
    stride = blk_count // SPAN
    def index_of(role, place, level, at):
        core = role ^ (2 * at // stride)
        return (2 * level + core) * blk_count + place * stride + at

    spots = [(p, z, at) for p in range(SPAN) for z in range(SPAN) for at in range(stride)]

    def swapped(value, over_x, over_z):
        pairs = []
        for p, z, at in spots:
            pairs.append((index_of(0, p, z, at), index_of(0, over_x(p), z, at)))
            pairs.append((index_of(1, p, z, at), index_of(1, p, over_z(z), at)))
        return lax.ppermute(value, AXES, pairs)

    mate = lambda at: at ^ 1
    mirror = lambda at: SPAN - 1 - at

    def level_shift(value, shift):
        pairs = [
            (index_of(1, p, p, at), index_of(1, p, (p + shift) % SPAN, at))
            for p in range(SPAN)
            for at in range(stride)
        ]
        return lax.ppermute(value, AXES, pairs)

    core_groups = [sorted(index_of(role, p, z, at) for role in range(2)) for p, z, at in spots]
    over_z = lambda role: [
        [index_of(role, p, z, at) for z in range(SPAN)] for p in range(SPAN) for at in range(stride)
    ]
    over_x = lambda role: [
        [index_of(role, p, z, at) for p in range(SPAN)] for z in range(SPAN) for at in range(stride)
    ]
    head_groups = over_z(0) + over_x(1)

    def exchanged(value, groups):
        return lax.all_to_all(
            value, AXES, split_axis=0, concat_axis=0, axis_index_groups=groups, tiled=True
        )

    side = (OWNERS, ROWS, HEAD_DIM)
    lse = logsumexp.reshape(OWNERS, ROWS)
    tokens = [
        pltpu.with_memory_space_constraint(value, pltpu.HBM)
        for value in (queries, key_rows, value_rows, attn_output, grad_output, positions)
    ]
    packed, table = call(
        pack_kernel,
        tokens,
        [HBM] * 6,
        [((2, SPAN, PART, HEAD_DIM), bf16), ((24,), jnp.int32)],
        [
            pltpu.VMEM((HEADS, ROWS, HEAD_DIM), bf16),
            pltpu.SMEM((SPAN, 128), jnp.int32),
            pltpu.SemaphoreType.DMA((5, HEADS)),
            pltpu.SemaphoreType.DMA((SPAN,)),
        ],
        name="pack",
        spaces=[VMEM, SMEM],
    )
    (slots,) = call(
        arrange_kernel,
        (exchanged(packed, core_groups), lse),
        [VMEM] * 2,
        [((SPAN, 2, PART, HEAD_DIM), bf16)],
        name="arrange",
    )
    card = ((OWNERS, 272, HEAD_DIM), bf16)
    rows = [row_scratch(), row_scratch()]
    query_side, key_side, first_out, second_out, run_lse = call(
        split_kernel,
        (table, exchanged(slots, head_groups), lse),
        [SMEM] + [VMEM] * 2,
        [card] * 4 + [((SPAN, OWNERS, ROWS), f32)],
        name="split",
    )
    first = swapped(first_out, mirror, mate)
    second = swapped(second_out, mate, mirror)
    cost = 10 * 128 * 2 * 512 * 512
    late_positions, _ = lax.optimization_barrier((positions, run_lse))
    first_places = lax.slice(late_positions, (0,), positions.shape, (OWNERS * ROWS,))
    flag = jnp.max(first_places).reshape(1)
    (given,) = call(
        lse_kernel,
        (table, run_lse, *(level_shift(run_lse, shift) for shift in range(1, SPAN))),
        [SMEM] + [VMEM] * 4,
        [((3, OWNERS, ROWS), f32)],
        name="lse",
    )
    grad_query, grad_key, grad_value, first_sum, first_value = call(
        first_kernel,
        (table, query_side, key_side, first, given),
        [SMEM] + [VMEM] * 4,
        [(side, f32)] * 5,
        rows,
        flops=cost,
        name="first",
    )
    grad_key, grad_value, query_sum, far_back = call(
        second_kernel,
        (table, key_side, first, second, given, grad_key, grad_value, first_sum, first_value),
        [SMEM] + [VMEM] * 8,
        [(side, f32)] * 3 + [((2,) + side, bf16)],
        [pltpu.VMEM(side, f32), pltpu.VMEM(side, f32)] + rows,
        flops=cost,
        name="second",
    )
    far_back = swapped(far_back, mirror, mirror)
    grad_key, grad_value, query_back = call(
        third_kernel,
        (table, key_side, second, grad_key, grad_value, query_sum),
        [SMEM] + [VMEM] * 5,
        [(side, f32)] * 2 + [(side, bf16)],
        [pltpu.VMEM(side, f32)] + rows,
        flops=4 * cost,
        name="third",
    )
    query_back = swapped(query_back, mate, mate)
    grad_query, grad_key, grad_value = call(
        own_kernel,
        (table, flag, query_side, key_side, given, grad_query, grad_key, grad_value),
        [SMEM] * 2 + [VMEM] * 6,
        [(side, f32)] * 3,
        rows,
        flops=1,
        moved=1,
        name="own",
    )
    def rising():
        (joined,) = call(
            join_kernel,
            (table, grad_query, grad_key, grad_value, query_back, far_back),
            [SMEM] + [VMEM] * 5,
            [((SPAN, 2, 3 * ROWS, HEAD_DIM), bf16)],
            name="join",
        )
        (turned,) = call(
            turn_kernel,
            (exchanged(joined, head_groups),),
            [VMEM],
            [((2, SPAN, 3 * ROWS, HEAD_DIM), bf16)],
            name="turn",
        )
        return tuple(
            call(
                unpack_kernel,
                (exchanged(turned, core_groups),),
                [VMEM],
                [((ROWS, HEADS * HEAD_DIM), bf16)] * 3,
                [pltpu.SemaphoreType.DMA((3, HEADS))],
                name="unpack",
                spaces=[HBM] * 3,
            )
        )

    def falling():
        return any_order(
            queries, key_rows, value_rows, attn_output, grad_output, logsumexp, positions
        )

    return lax.cond(flag[0] >= SPAN * 2 * CHUNK, falling, rising)


def solution(mesh):
    tokens = P(("blk", "ulysses"), None)
    return jax.shard_map(
        per_device,
        mesh=mesh,
        in_specs=(tokens,) * 5 + (P("blk", "ulysses"), P()),
        out_specs=(tokens,) * 3,
        check_vma=False,
    )
```
